512 devices in a mesh: dp: 32 (over y, x, core), tensor: 16 (over z).
Axes of the slice: x: 4, y: 4, z: 16, core: 2. Of those that a mesh axis runs over, the one named last changes fastest.
Arguments:
- grad_out: bfloat16 [32, 256, 3072], P('dp', 'tensor'), may hold values from -6 to 6
- hidden: bfloat16 [32, 256, 12288], P('dp', None, 'tensor'), may hold values from -6 to 6
- error: bfloat16 [32, 3072, 12288], P('dp', None, 'tensor'), may hold values from -96 to 96
- q_init: float32 [12288, 32], P('tensor'), may hold values from -6 to 6
Outputs:
- basis: float32 [3072, 32], P('tensor')
- q_new: float32 [12288, 32], P('tensor')
The draws below stay inside these ranges and needn't reach their ends.
All inputs are finite; a program needn't handle non-finite values.
Results may differ from the reference program's by a relative error of at most 0.0003.
Values may be sent and summed in bfloat16 or wider, within the bound.
A program may use at most 64 MiB of HBM per device.

```python
import jax
import jax.numpy as jnp
from jax import lax

D = 3072
FF = 12288
R = 32
TOK = 256
N_DP = 32


def shard_levels(own_key, shape, cuts, low, largest):
    def one(axis_at, parts):
        heights = jax.random.uniform(jax.random.fold_in(jax.random.fold_in(own_key, 6), axis_at), (parts,), jnp.float32, low / len(cuts), largest / len(cuts))
        return jnp.repeat(jnp.exp(heights), shape[axis_at] // parts).reshape((-1,) + (1,) * (len(shape) - axis_at - 1))

    factor_of = one(*cuts[0])
    for cut in cuts[1:]:
        factor_of = factor_of * one(*cut)
    return factor_of


def noise(own_key, dims, spread, reach, split=(), dtype=jnp.bfloat16):
    drawn = jax.random.normal(own_key, dims, jnp.float32) * spread
    if len(split) > 0:
        drawn = shard_levels(own_key, dims, split, -0.22, 0.18) * drawn
    return jnp.clip(drawn, min=-reach, max=reach).astype(dtype)


def setup_inputs(seed: int = 0) -> dict:
    key_of = jax.random.split(jax.random.key(seed), 5)
    return {
        "grad_out": noise(key_of[0], (N_DP, TOK, D), 1.0, 6.0, ((0, 32), (1, 16))),
        "hidden": noise(key_of[1], (N_DP, TOK, FF), 1.0, 6.0, ((0, 32), (2, 16))),
        "error": noise(key_of[2], (N_DP, D, FF), (TOK ** 0.5), 96.0, ((0, 32), (2, 16))),
        "q_init": noise(key_of[3], (FF, R), 1.0, 6.0, ((0, 16),), jnp.float32),
    }


def reference(grad_out, hidden, error, q_init):
    high = lax.Precision.HIGHEST
    width = grad_out.shape[2]
    rank = q_init.shape[1]

    def sketch_step(total, item):
        grads, acts, memory = item
        images = jnp.dot(acts.astype(jnp.float32), q_init, precision=high)
        term = jnp.einsum('td,tr->dr', grads.astype(jnp.float32), images, precision=high)
        term = term + jnp.dot(memory.astype(jnp.float32), q_init, precision=high)
        return (total + term, None)
    p_total, unused = lax.scan(sketch_step, jnp.zeros((width, rank), jnp.float32), (grad_out, hidden, error))
    gram = jnp.dot(p_total.T, p_total, precision=high)
    lower = jnp.linalg.cholesky(gram)
    p_hat = lax.linalg.triangular_solve(lower, p_total, left_side=False, lower=True, transpose_a=True)

    def coeff_step(total, item):
        grads, acts, memory = item
        weights = jnp.dot(grads.astype(jnp.float32), p_hat, precision=high)
        term = jnp.einsum('tf,tr->fr', acts.astype(jnp.float32), weights, precision=high)
        term = term + jnp.einsum('df,dr->fr', memory.astype(jnp.float32), p_hat, precision=high)
        return (total + term, None)
    q_total, unused = lax.scan(coeff_step, jnp.zeros((q_init.shape[0], rank), jnp.float32), (grad_out, hidden, error))
    basis = p_hat * jnp.sqrt(jnp.float32(width))
    return (basis, q_total / N_DP)
```

```python
import functools

import jax
import jax.numpy as jnp
from jax import lax
from jax.experimental import pallas as pl
from jax.experimental.pallas import tpu as pltpu
from jax.sharding import PartitionSpec as P

MESH = pl.DeviceIdType.MESH
NT = (((1,), (1,)), ((), ()))
NN = (((1,), (0,)), ((), ()))
F32, BF16 = jnp.float32, jnp.bfloat16
HIGH = lax.Precision.HIGHEST

NZ, CHIPS, DP = 16, 16, 32
D, F, R, TOK = 3072, 768, 32, 256
LANES, HALF, QUART = 128, 384, 768
SCALE = 2.0**20
OWNERS = [(4 * y + x) * 2 + c for y in range(4) for x in range(4) if x != y for c in range(2)]
TILES = len(OWNERS)


def dot(a, b, dims):
    return lax.dot_general(a, b, dims, preferred_element_type=F32)


def split(v):
    hi = v.astype(BF16)
    return hi, (v - hi.astype(F32)).astype(BF16)


def take(ref, sem):
    pltpu.make_async_copy(ref, ref, sem).wait()


def aligned(i, n):
    return pl.multiple_of(i, n)


def inverse_factor(gram):
    row = lax.broadcasted_iota(jnp.int32, (R, 2 * R), 0)
    col = lax.broadcasted_iota(jnp.int32, (R, 2 * R), 1)
    one = (col - R == row).astype(F32)
    a = jnp.concatenate([gram, one[:, R:]], axis=1)
    for k in range(R):
        pivot = a[k : k + 1, :]
        step = jnp.where(row[:, :1] > k, a[:, k : k + 1] / a[k : k + 1, k : k + 1], 0.0)
        a = a - step * pivot
    diag = jnp.sum(jnp.where(row == col, a, 0.0), axis=1, keepdims=True)
    return a[:, R:] / jnp.sqrt(diag)


def kernel(
    grad_hbm, hid_hbm, err_hbm, qt_hbm, basis_ref, qnew_ref,
    grad, hid, err, qt, hidp, pt, img_send, img_recv, core_recv, rs_send, rs_recv,
    red, zrecv, ptf, wrecv, s_send, s_recv, fin, linv,
    loc, img_s, img_r, core_s, core_r, rs_s, rs_r, zrs_s, zrs_r, zag_s, zag_r,
    ag_s, ag_r, fwd_s, fwd_r, w_s, w_r, srs_s, srs_r, sag_s, sag_r,
):
    dp = lax.axis_index("dp")
    z = lax.axis_index("tensor")
    core, chip = dp % 2, dp // 2
    x, y = chip % 4, chip // 4
    sibling = dp + 1 - 2 * core

    def send(src, dst, s, r, to):
        copy = pltpu.make_async_remote_copy(
            src_ref=src, dst_ref=dst, send_sem=s, recv_sem=r,
            device_id=to, device_id_type=MESH,
        )
        copy.start()

    loads = [
        pltpu.make_async_copy(qt_hbm, qt, loc.at[0]),
        pltpu.make_async_copy(hid_hbm, hid, loc.at[1]),
    ]
    loads += [
        pltpu.make_async_copy(
            err_hbm.at[pl.ds(c * QUART, QUART)], err.at[pl.ds(c * QUART, QUART)], loc.at[3 + c]
        )
        for c in range(4)
    ]
    loads.insert(2, pltpu.make_async_copy(grad_hbm, grad, loc.at[2]))
    for load in loads:
        load.start()

    barrier = pltpu.get_barrier_semaphore()
    for d in range(1, DP):
        pl.semaphore_signal(barrier, 1, device_id=((dp + d) % DP, z), device_id_type=MESH)
    for d in range(1, NZ):
        pl.semaphore_signal(barrier, 1, device_id=(dp, (z + d) % NZ), device_id_type=MESH)

    lane = lax.broadcasted_iota(jnp.int32, (8, LANES), 1)
    sends = []

    def finish():
        for fn in sends:
            fn()


    loads[0].wait()
    q_hi, q_lo = split(qt[...])
    q2 = jnp.concatenate([q_hi, q_lo], axis=0)
    loads[1].wait()
    images = dot(hid[...], jnp.concatenate([q2, q2], axis=0), NT).reshape(NZ, 2, 8, LANES)
    img_send[...] = jnp.where((lane < 2 * R)[None], images[:, 0], images[:, 1])
    loads[2].wait()
    pl.semaphore_wait(barrier, DP + NZ - 2)
    for d in range(1, NZ):
        to = (z + d) % NZ
        send(img_send.at[to], img_recv.at[d - 1], img_s, img_r, (dp, to))
    sends.append(lambda: take(img_send.at[pl.ds(0, NZ - 1)], img_s))

    for c in range(4):
        loads[3 + c].wait()
        part = dot(q2, err[pl.ds(c * QUART, QUART), :], NT)
        pt[:, pl.ds(c * QUART, QUART)] = part[:R] + part[R:]
    by_tile = hid[...].astype(F32).reshape(NZ, 2, 8, F)
    hidp[...] = jnp.concatenate([by_tile[:, 0], by_tile[:, 1]], axis=0).reshape(TOK, F).astype(BF16)

    take(img_recv, img_r)
    own = jnp.sum(img_recv[...], axis=0) + img_send[z]
    own = own.T
    own = jnp.concatenate([own[:R] + own[R : 2 * R], own[2 * R : 3 * R] + own[3 * R :]], axis=1)
    im_hi, im_lo = split(own)
    im2 = jnp.concatenate([im_hi, im_lo], axis=0)
    for c in range(4):
        cols = pl.ds(c * QUART, QUART)
        part = dot(im2, grad[:, cols], NN)
        pt[:, cols] += part[:R] + part[R:]
        theirs = pl.ds(aligned(c * QUART + (1 - core) * HALF, LANES), HALF)
        send(pt.at[:, theirs], core_recv.at[c], core_s, core_r.at[c], (sibling, z))
    sends.append(lambda: take(core_recv, core_s))

    for c in range(4):
        take(core_recv.at[c], core_r.at[c])
        mine = pt[:, pl.ds(aligned(c * QUART + core * HALF, LANES), HALF)] + core_recv[c]
        for g in range(4):
            t = 4 * c + g
            rs_send[t] = mine[8 * g : 8 * g + 8]

            @pl.when(t != chip)
            def _(t=t):
                send(rs_send.at[t], rs_recv.at[chip], rs_s, rs_r, (2 * t + core, z))

    sends.append(lambda: take(rs_send.at[pl.ds(0, CHIPS - 1)], rs_s))
    rs_recv[chip] = rs_send[chip]
    take(rs_recv.at[pl.ds(0, CHIPS - 1)], rs_r)
    red[...] = jnp.sum(rs_recv[...], axis=0)

    rows = pl.ds(aligned(8 * x, 8), 8)
    base = y * QUART + core * HALF
    place = [5 * t + 8 * core for t in range(3)]
    place = [lax.rem(p, NZ) for p in place]
    tile_at = [ptf.at[rows, pl.ds(aligned(base + t * LANES, LANES), LANES)] for t in range(3)]
    for t in range(3):

        @pl.when(z != place[t])
        def _(t=t):
            send(red.at[:, pl.ds(t * LANES, LANES)], zrecv.at[z], zrs_s, zrs_r, (dp, place[t]))

    for t in range(3):

        @pl.when(z == place[t])
        def _(t=t):
            zrecv[z] = red[:, t * LANES : (t + 1) * LANES]
            take(zrecv.at[pl.ds(0, NZ - 1)], zrs_r)
            tile_at[t][...] = jnp.sum(zrecv[...], axis=0) * SCALE
            for d in range(1, NZ):
                send(tile_at[t], tile_at[t], zag_s, zag_r.at[t], (dp, (z + d) % NZ))

    for t in range(3):

        @pl.when(z != place[t])
        def _(t=t):
            take(tile_at[t], zag_r.at[t])

    def z_sends():
        for t in range(3):

            @pl.when(z == place[t])
            def _():
                take(red.at[:, pl.ds(0, 2 * LANES)], zrs_s)
                take(zrecv.at[pl.ds(0, NZ - 1)], zag_s)

        @pl.when((z != place[0]) & (z != place[1]) & (z != place[2]))
        def _():
            take(red, zrs_s)

    sends.append(z_sends)

    window = ptf.at[rows, pl.ds(aligned(base, LANES), HALF)]
    for d in range(1, CHIPS):
        send(window, window, ag_s, ag_r.at[chip], (2 * ((chip + d) % CHIPS) + core, z))
    sends.append(lambda: take(rs_send.at[pl.ds(0, CHIPS - 1)], ag_s))
    for dy in range(4):
        yy = (y + dy) % 4
        for dx in range(1 if dy == 0 else 0, 4):
            xx = (x + dx) % 4
            there = ptf.at[
                pl.ds(aligned(8 * xx, 8), 8), pl.ds(aligned(yy * QUART + core * HALF, LANES), HALF)
            ]
            take(there, ag_r.at[4 * yy + xx])
        block = ptf.at[:, pl.ds(aligned(yy * QUART + core * HALF, LANES), HALF)]
        send(block, block, fwd_s, fwd_r, (sibling, z))
    sends.append(lambda: take(core_recv, fwd_s))
    take(core_recv, fwd_r)

    p_hi, p_lo = split(ptf[...])
    p2 = jnp.concatenate([p_hi, p_lo], axis=0)
    w = dot(grad[...], jnp.concatenate([p2, p2], axis=0), NT)
    wrecv[z] = jnp.where(lane < 2 * R, w[:8], w[8:])
    for d in range(1, NZ):
        send(wrecv.at[z], wrecv.at[z], w_s, w_r, (dp, (z + d) % NZ))
    sends.append(lambda: take(wrecv.at[pl.ds(0, NZ - 1)], w_s))

    part = dot(p2, err[...], NN)
    s_err = part[:R] + part[R:]
    gram = dot(p2, p2, NT)
    gram = gram[:R, :R] + gram[R:, R:] + (gram[:R, R:] + gram[R:, :R])

    take(wrecv.at[pl.ds(0, NZ - 1)], w_r)
    wt = wrecv[...].reshape(LANES, LANES).T
    wt = jnp.concatenate([wt[:R] + wt[R : 2 * R], wt[2 * R : 3 * R] + wt[3 * R :]], axis=1)
    w_hi, w_lo = split(wt)
    part = dot(jnp.concatenate([w_hi, w_lo], axis=0), hidp[...], NN)
    s = s_err + part[:R] + part[R:]

    for t, owner in enumerate(OWNERS):
        g, k = t // 6, t % 6
        s_send[t] = s[8 * g : 8 * g + 8, k * LANES : (k + 1) * LANES]

        @pl.when(dp != owner)
        def _(t=t, owner=owner):
            send(s_send.at[t], s_recv.at[dp], srs_s, srs_r, (owner, z))

    linv[...] = inverse_factor(gram)
    first = aligned((3 * z) // 2 * LANES, LANES)
    near = ptf[:, pl.ds(first, 2 * LANES)]
    near = jnp.where(z % 2 == 1, near[:, 64:], near[:, :192])
    basis_ref[...] = jnp.dot(linv[...], near, precision=HIGH, preferred_element_type=F32) * (
        float(D) ** 0.5
    )

    is_owner = x != y
    tile = (3 * y + x - (x > y).astype(jnp.int32)) * 2 + core
    g, k = tile // 6, tile % 6
    here = fin.at[pl.ds(aligned(8 * g, 8), 8), pl.ds(aligned(k * LANES, LANES), LANES)]

    @pl.when(is_owner)
    def _():
        s_recv[dp] = s_send[tile]
        take(s_recv.at[pl.ds(0, DP - 1)], srs_r)
        here[...] = jnp.sum(s_recv[...], axis=0)
        for d in range(1, DP):
            send(here, here, sag_s, sag_r, ((dp + d) % DP, z))
        take(s_send.at[pl.ds(0, TILES - 1)], sag_r)

    @pl.when(jnp.logical_not(is_owner))
    def _():
        take(s_send, sag_r)

    def s_sends():
        @pl.when(is_owner)
        def _():
            take(s_send.at[pl.ds(0, TILES - 1)], srs_s)
            take(s_recv.at[pl.ds(0, DP - 1)], sag_s)

        @pl.when(jnp.logical_not(is_owner))
        def _():
            take(s_send, srs_s)

    sends.append(s_sends)
    qnew_ref[...] = jnp.dot(linv[...], fin[...], precision=HIGH, preferred_element_type=F32) * (
        1.0 / DP
    )
    finish()


def body(grad_out, hidden, error, q_init):
    one, many = pltpu.SemaphoreType.DMA, lambda n: pltpu.SemaphoreType.DMA((n,))
    vmem = pltpu.VMEM
    basis, q_new = pl.pallas_call(
        kernel,
        out_shape=(
            jax.ShapeDtypeStruct((R, D // NZ), F32),
            jax.ShapeDtypeStruct((R, F), F32),
        ),
        in_specs=[pl.BlockSpec(memory_space=pltpu.HBM)] * 4,
        out_specs=[pl.BlockSpec(memory_space=pltpu.VMEM)] * 2,
        scratch_shapes=[
            vmem((TOK // NZ, D), BF16),
            vmem((TOK, F), BF16),
            vmem((D, F), BF16),
            vmem((R, F), F32),
            vmem((TOK, F), BF16),
            vmem((R, D), F32),
            vmem((NZ, 8, LANES), F32),
            vmem((NZ - 1, 8, LANES), F32),
            vmem((4, R, HALF), F32),
            vmem((CHIPS, 8, HALF), F32),
            vmem((CHIPS, 8, HALF), F32),
            vmem((8, HALF), F32),
            vmem((NZ, 8, LANES), F32),
            vmem((R, D), F32),
            vmem((NZ, 8, LANES), F32),
            vmem((TILES, 8, LANES), F32),
            vmem((DP, 8, LANES), F32),
            vmem((R, F), F32),
            vmem((R, R), F32),
            many(7),
            one, one,
            one, many(4),
            one, one,
            one, one,
            one, many(3),
            one, many(CHIPS),
            one, one,
            one, one,
            one, one,
            one, one,
        ],
        compiler_params=pltpu.CompilerParams(
            collective_id=0, has_side_effects=True, vmem_limit_bytes=60 * 1024 * 1024
        ),
    )(grad_out[0], hidden[0], error[0], q_init.T)
    return basis.T, q_new.T


def solution(mesh):
    return jax.shard_map(
        body,
        mesh=mesh,
        in_specs=(
            P("dp", "tensor", None),
            P("dp", None, "tensor"),
            P("dp", None, "tensor"),
            P("tensor", None),
        ),
        out_specs=(P("tensor", None), P("tensor", None)),
        check_vma=False,
    )
```

```python
import functools

import jax
import jax.numpy as jnp
from jax import lax
from jax.experimental import pallas as pl
from jax.experimental.pallas import tpu as pltpu
from jax.sharding import PartitionSpec as P

MESH = pl.DeviceIdType.MESH
NT = (((1,), (1,)), ((), ()))
NN = (((1,), (0,)), ((), ()))
F32, BF16 = jnp.float32, jnp.bfloat16
HIGH = lax.Precision.HIGHEST

NZ, CHIPS, DP = 16, 16, 32
D, F, R, TOK = 3072, 768, 32, 256
LANES, HALF, QUART = 128, 384, 768
FAR_Z = sorted(range(1, NZ), key=lambda d: -min(d, NZ - d))
FAR_XY = sorted(range(1, CHIPS), key=lambda d: -min(d % 4, 4 - d % 4) - min(d // 4, 4 - d // 4))
SCALE = 2.0**20
BLOCK = TOK // NZ


def dot(a, b, dims):
    return lax.dot_general(a, b, dims, preferred_element_type=F32)


def split(v):
    hi = v.astype(BF16)
    return hi, (v - hi.astype(F32)).astype(BF16)


def take(ref, sem):
    pltpu.make_async_copy(ref, ref, sem).wait()


def aligned(i, n):
    return pl.multiple_of(i, n)


def sum_terms(v):
    return v + pltpu.roll(v, R, 1)


def pack(v):
    quarter = lax.broadcasted_iota(jnp.int32, (1, LANES), 1) // R
    v = jnp.where(quarter < 2, v[..., :8, :], v[..., 8:, :])
    return jnp.where(quarter % 2 == 0, v[..., :4, :], v[..., 4:, :])


def unpack(v):
    v = v.T
    return jnp.concatenate([v[R * g : R * g + R] for g in range(4)], axis=1)


def inverse_factor(gram):
    row = lax.broadcasted_iota(jnp.int32, (R, 2 * R), 0)
    col = lax.broadcasted_iota(jnp.int32, (R, 2 * R), 1)
    one = (col - R == row).astype(F32)
    a = jnp.concatenate([gram, one[:, R:]], axis=1)
    for k in range(R):
        pivot = a[k : k + 1, :]
        step = jnp.where(row[:, :1] > k, a[:, k : k + 1] / a[k : k + 1, k : k + 1], 0.0)
        a = a - step * pivot
    diag = jnp.sum(jnp.where(row == col, a, 0.0), axis=1, keepdims=True)
    return a[:, R:] / jnp.sqrt(diag)


def kernel(
    grad_hbm, hid_hbm, err_hbm, qt_hbm, basis_ref, qnew_ref,
    grad, hid, err, qt, hidp, pt, img_send, img_recv, core_recv, rs_send, rs_recv,
    red, znext, zrecv, ptf, wrecv, s_buf, s_core, sx, sy, sx2, sy2, linv,
    loc, img_s, img_r, core_s, core_r, rs_s, rs_r, zn_s, zn_r, z_s, z_r,
    ag_s, ag_r, fwd_s, fwd_r, w_s, w_r, sc_s, sc_r, sx_s, sx_r, sy_s, sy_r,
    sx2_s, sx2_r, sy2_s, sy2_r, q_s, q_r,
):
    dp = lax.axis_index("dp")
    z = lax.axis_index("tensor")
    core, chip = dp % 2, dp // 2
    x, y = chip % 4, chip // 4
    sibling = dp + 1 - 2 * core

    def chip_at(d):
        return 2 * (4 * ((y + d // 4) % 4) + (x + d % 4) % 4) + core

    def send(src, dst, s, r, to):
        copy = pltpu.make_async_remote_copy(
            src_ref=src, dst_ref=dst, send_sem=s, recv_sem=r,
            device_id=to, device_id_type=MESH,
        )
        copy.start()

    loads = [
        pltpu.make_async_copy(qt_hbm, qt, loc.at[0]),
        pltpu.make_async_copy(hid_hbm, hid, loc.at[1]),
    ]
    loads += [
        pltpu.make_async_copy(
            err_hbm.at[pl.ds(c * QUART, QUART)], err.at[pl.ds(c * QUART, QUART)], loc.at[3 + c]
        )
        for c in range(4)
    ]
    loads.insert(2, pltpu.make_async_copy(grad_hbm, grad, loc.at[2]))
    for load in loads:
        load.start()

    barrier = pltpu.get_barrier_semaphore()
    pl.semaphore_signal(barrier, 1, device_id=(sibling, z), device_id_type=MESH)
    for d in FAR_XY:
        to = chip_at(d)
        pl.semaphore_signal(barrier, 1, device_id=(to, z), device_id_type=MESH)
    for d in FAR_Z:
        pl.semaphore_signal(barrier, 1, device_id=(dp, (z + d) % NZ), device_id_type=MESH)

    sends = []

    def finish():
        for fn in sends:
            fn()


    loads[0].wait()
    q_hi, q_lo = split(qt[...])
    q2 = jnp.concatenate([q_hi, q_lo], axis=0)
    loads[1].wait()
    images = sum_terms(dot(hid[...], jnp.concatenate([q2, q2], axis=0), NT))
    img_send[...] = pack(images.reshape(NZ, BLOCK, LANES))
    loads[2].wait()
    pl.semaphore_wait(barrier, CHIPS + NZ - 1)
    for d in FAR_Z:
        to = (z + d) % NZ
        send(img_send.at[to], img_recv.at[d - 1], img_s, img_r, (dp, to))
    sends.append(lambda: take(img_send.at[pl.ds(0, NZ - 1)], img_s))

    for c in range(4):
        loads[3 + c].wait()
        part = dot(q2, err[pl.ds(c * QUART, QUART), :], NT)
        pt[:, pl.ds(c * QUART, QUART)] = part[:R] + part[R:]
    by_quarter = hid[...].astype(F32).reshape(NZ, 4, 4, F)
    by_quarter = [by_quarter[:, g].reshape(TOK // 4, F) for g in range(4)]
    hidp[...] = jnp.concatenate(by_quarter, axis=0).astype(BF16)

    take(img_recv, img_r)
    im_hi, im_lo = split(unpack(jnp.sum(img_recv[...], axis=0) + img_send[z]))
    im2 = jnp.concatenate([im_hi, im_lo], axis=0)
    for c in range(4):
        cols = pl.ds(c * QUART, QUART)
        part = dot(im2, grad[:, cols], NN)
        pt[:, cols] += part[:R] + part[R:]
        theirs = pl.ds(aligned(c * QUART + (1 - core) * HALF, LANES), HALF)
        send(pt.at[:, theirs], core_recv.at[c], core_s, core_r.at[c], (sibling, z))
    sends.append(lambda: take(core_recv, core_s))

    for c in range(4):
        take(core_recv.at[c], core_r.at[c])
        mine = pt[:, pl.ds(aligned(c * QUART + core * HALF, LANES), HALF)] + core_recv[c]
        for g in range(4):
            t = 4 * c + g
            rs_send[t] = mine[8 * g : 8 * g + 8]

            @pl.when(t != chip)
            def _(t=t):
                send(rs_send.at[t], rs_recv.at[chip], rs_s, rs_r, (2 * t + core, z))

    sends.append(lambda: take(rs_send.at[pl.ds(0, CHIPS - 1)], rs_s))
    rs_recv[chip] = rs_send[chip]
    take(rs_recv.at[pl.ds(0, CHIPS - 1)], rs_r)
    red[...] = jnp.sum(rs_recv[...], axis=0)

    rows = pl.ds(aligned(8 * x, 8), 8)
    base = y * QUART + core * HALF
    window = ptf.at[rows, pl.ds(aligned(base, LANES), HALF)]
    send(red, znext, zn_s, zn_r, (dp, (z + NZ - 1) % NZ))
    sends.append(lambda: take(red, zn_s))
    take(znext, zn_r)
    pair = z // 2
    zrecv[pair] = red[...] + znext[...]
    for d in FAR_Z:
        if d % 2:
            continue
        send(zrecv.at[pair], zrecv.at[pair], z_s, z_r, (dp, (z + d) % NZ))
    others = zrecv.at[pl.ds(0, NZ // 2 - 1)]
    sends.append(lambda: take(others, z_s))
    take(others, z_r)
    window[...] = jnp.sum(zrecv[...], axis=0) * SCALE

    for d in FAR_XY:
        send(window, window, ag_s, ag_r.at[chip], (chip_at(d), z))
    sends.append(lambda: take(rs_send.at[pl.ds(0, CHIPS - 1)], ag_s))
    for dy in range(4):
        yy = (y + dy) % 4
        for dx in range(1 if dy == 0 else 0, 4):
            xx = (x + dx) % 4
            there = ptf.at[
                pl.ds(aligned(8 * xx, 8), 8), pl.ds(aligned(yy * QUART + core * HALF, LANES), HALF)
            ]
            take(there, ag_r.at[4 * yy + xx])
        block = ptf.at[:, pl.ds(aligned(yy * QUART + core * HALF, LANES), HALF)]
        send(block, block, fwd_s, fwd_r, (sibling, z))
    sends.append(lambda: take(core_recv, fwd_s))
    take(core_recv, fwd_r)

    p_hi, p_lo = split(ptf[...])
    p2 = jnp.concatenate([p_hi, p_lo], axis=0)
    w = dot(grad[...], jnp.concatenate([p2, p2], axis=0), NT)
    wrecv[z] = pack(sum_terms(w))
    for d in FAR_Z:
        send(wrecv.at[z], wrecv.at[z], w_s, w_r, (dp, (z + d) % NZ))
    sends.append(lambda: take(wrecv.at[pl.ds(0, NZ - 1)], w_s))

    part = dot(p2, err[...], NN)
    s_err = part[:R] + part[R:]
    gram = dot(p2, p2, NT)
    gram = gram[:R, :R] + gram[R:, R:] + (gram[:R, R:] + gram[R:, :R])

    linv[...] = inverse_factor(gram)
    first = aligned((3 * z) // 2 * LANES, LANES)
    near = ptf[:, pl.ds(first, 2 * LANES)]
    near = jnp.where(z % 2 == 1, near[:, 64:], near[:, :192])
    basis_ref[...] = jnp.dot(linv[...], near, precision=HIGH, preferred_element_type=F32) * (
        float(D) ** 0.5
    )

    take(wrecv.at[pl.ds(0, NZ - 1)], w_r)
    w_hi, w_lo = split(unpack(wrecv[...].reshape(TOK // 4, LANES)))
    part = dot(jnp.concatenate([w_hi, w_lo], axis=0), hidp[...], NN)
    s_buf[...] = s_err + part[:R] + part[R:]

    my_cols = pl.ds(aligned(core * HALF, LANES), HALF)
    their_cols = pl.ds(aligned((1 - core) * HALF, LANES), HALF)
    send(s_buf.at[:, their_cols], s_core, sc_s, sc_r, (sibling, z))
    sends.append(lambda: take(s_core, sc_s))
    take(s_core, sc_r)
    mine = s_buf[:, my_cols] + s_core[...]

    def exchange(along_x, along_y, sx_s, sx_r, sy_s, sy_r):
        for d in range(1, 4):
            to = 2 * (4 * y + (x + d) % 4) + core
            send(along_x.at[x], along_x.at[x], sx_s, sx_r, (to, z))
            to = 2 * (4 * ((y + d) % 4) + x) + core
            send(along_y.at[y], along_y.at[y], sy_s, sy_r, (to, z))
        sends.append(lambda: take(along_x.at[pl.ds(0, 3)], sx_s))
        sends.append(lambda: take(along_y.at[pl.ds(0, 3)], sy_s))

    sx[x] = mine[: R // 2]
    sy[y] = mine[R // 2 :]
    exchange(sx, sy, sx_s, sx_r, sy_s, sy_r)

    take(sx.at[pl.ds(0, 3)], sx_r)
    take(sy.at[pl.ds(0, 3)], sy_r)
    sy2[y] = jnp.sum(sx[...], axis=0)
    sx2[x] = jnp.sum(sy[...], axis=0)
    exchange(sx2, sy2, sx2_s, sx2_r, sy2_s, sy2_r)
    take(sx2.at[pl.ds(0, 3)], sx2_r)
    take(sy2.at[pl.ds(0, 3)], sy2_r)
    s = jnp.concatenate([jnp.sum(sy2[...], axis=0), jnp.sum(sx2[...], axis=0)], axis=0)
    my_q = qnew_ref.at[:, my_cols]
    my_q[...] = jnp.dot(linv[...], s, precision=HIGH, preferred_element_type=F32) * (1.0 / DP)
    send(my_q, my_q, q_s, q_r, (sibling, z))
    sends.append(lambda: take(s_core, q_s))
    take(qnew_ref.at[:, their_cols], q_r)
    finish()


def body(grad_out, hidden, error, q_init):
    one, many = pltpu.SemaphoreType.DMA, lambda n: pltpu.SemaphoreType.DMA((n,))
    vmem = pltpu.VMEM
    basis, q_new = pl.pallas_call(
        kernel,
        out_shape=(
            jax.ShapeDtypeStruct((R, D // NZ), F32),
            jax.ShapeDtypeStruct((R, F), F32),
        ),
        in_specs=[pl.BlockSpec(memory_space=pltpu.HBM)] * 4,
        out_specs=[pl.BlockSpec(memory_space=pltpu.VMEM)] * 2,
        scratch_shapes=[
            vmem((TOK // NZ, D), BF16),
            vmem((TOK, F), BF16),
            vmem((D, F), BF16),
            vmem((R, F), F32),
            vmem((TOK, F), BF16),
            vmem((R, D), F32),
            vmem((NZ, 4, LANES), F32),
            vmem((NZ - 1, 4, LANES), F32),
            vmem((4, R, HALF), F32),
            vmem((CHIPS, 8, HALF), F32),
            vmem((CHIPS, 8, HALF), F32),
            vmem((8, HALF), F32),
            vmem((8, HALF), F32),
            vmem((NZ // 2, 8, HALF), F32),
            vmem((R, D), F32),
            vmem((NZ, 4, LANES), F32),
            vmem((R, F), F32),
            vmem((R, HALF), F32),
            vmem((4, R // 2, HALF), F32),
            vmem((4, R // 2, HALF), F32),
            vmem((4, R // 2, HALF), F32),
            vmem((4, R // 2, HALF), F32),
            vmem((R, R), F32),
            many(7),
            one, one,
            one, many(4),
            one, one,
            one, one,
            one, one,
            one, many(CHIPS),
            one, one,
            one, one,
            one, one,
            one, one,
            one, one,
            one, one,
            one, one,
            one, one,
        ],
        compiler_params=pltpu.CompilerParams(
            collective_id=0, has_side_effects=True, vmem_limit_bytes=60 * 1024 * 1024
        ),
    )(grad_out[0], hidden[0], error[0], q_init.T)
    return basis.T, q_new.T


def solution(mesh):
    return jax.shard_map(
        body,
        mesh=mesh,
        in_specs=(
            P("dp", "tensor", None),
            P("dp", None, "tensor"),
            P("dp", None, "tensor"),
            P("tensor", None),
        ),
        out_specs=(P("tensor", None), P("tensor", None)),
        check_vma=False,
    )
```

```python
import functools

import jax
import jax.numpy as jnp
from jax import lax
from jax.experimental import pallas as pl
from jax.experimental.pallas import tpu as pltpu
from jax.sharding import PartitionSpec as P

MESH = pl.DeviceIdType.MESH
NT = (((1,), (1,)), ((), ()))
NN = (((1,), (0,)), ((), ()))
F32, BF16 = jnp.float32, jnp.bfloat16
HIGH = lax.Precision.HIGHEST

NZ, CHIPS, DP = 16, 16, 32
D, F, R, TOK = 3072, 768, 32, 256
LANES, HALF, QUART = 128, 384, 768
FAR = (2, 1, 3, 0)
FAR_Z = sorted(range(1, NZ), key=lambda d: -min(d, NZ - d))
FAR_XY = sorted(range(1, CHIPS), key=lambda d: -min(d % 4, 4 - d % 4) - min(d // 4, 4 - d // 4))
SCALE = 2.0**20
BLOCK = TOK // NZ


def dot(a, b, dims):
    return lax.dot_general(a, b, dims, preferred_element_type=F32)


def split(v):
    hi = v.astype(BF16)
    return hi, (v - hi.astype(F32)).astype(BF16)


def take(ref, sem):
    pltpu.make_async_copy(ref, ref, sem).wait()


def aligned(i, n):
    return pl.multiple_of(i, n)


def sum_terms(v):
    return v + pltpu.roll(v, R, 1)


def pack(v):
    quarter = lax.broadcasted_iota(jnp.int32, (1, LANES), 1) // R
    v = jnp.where(quarter < 2, v[..., :8, :], v[..., 8:, :])
    return jnp.where(quarter % 2 == 0, v[..., :4, :], v[..., 4:, :])


def unpack(v):
    v = v.T
    return jnp.concatenate([v[R * g : R * g + R] for g in range(4)], axis=1)


def inverse_factor(gram):
    row = lax.broadcasted_iota(jnp.int32, (R, 2 * R), 0)
    col = lax.broadcasted_iota(jnp.int32, (R, 2 * R), 1)
    one = (col - R == row).astype(F32)
    a = jnp.concatenate([gram, one[:, R:]], axis=1)
    for k in range(R):
        pivot = a[k : k + 1, :]
        step = jnp.where(row[:, :1] > k, a[:, k : k + 1] / a[k : k + 1, k : k + 1], 0.0)
        a = a - step * pivot
    diag = jnp.sum(jnp.where(row == col, a, 0.0), axis=1, keepdims=True)
    return a[:, R:] / jnp.sqrt(diag)


def kernel(
    grad_hbm, hid_hbm, err_hbm, qt_hbm, basis_ref, qnew_ref,
    grad, hid, err, qt, hidp, pt, img_send, img_recv, core_recv, rs_send, rs_recv,
    zrecv, ptf, wrecv, s_buf, s_core, sx, sy, sx2, sy2, linv,
    loc, img_s, img_r, core_s, core_r, rs_s, rs_r, z_s, z_r,
    ag_s, ag_r, fwd_s, fwd_r, w_s, w_r, sc_s, sc_r, sx_s, sx_r, sy_s, sy_r,
    sx2_s, sx2_r, sy2_s, sy2_r, q_s, q_r,
):
    dp = lax.axis_index("dp")
    z = lax.axis_index("tensor")
    core, chip = dp % 2, dp // 2
    x, y = chip % 4, chip // 4
    sibling = dp + 1 - 2 * core
    odd, pair = z % 2, z // 2
    partner = z + 1 - 2 * odd

    def chip_at(d):
        return 2 * (4 * ((y + d // 4) % 4) + (x + d % 4) % 4) + core

    def send(src, dst, s, r, to):
        copy = pltpu.make_async_remote_copy(
            src_ref=src, dst_ref=dst, send_sem=s, recv_sem=r,
            device_id=to, device_id_type=MESH,
        )
        copy.start()

    loads = [
        pltpu.make_async_copy(qt_hbm, qt, loc.at[0]),
        pltpu.make_async_copy(hid_hbm, hid, loc.at[1]),
    ]
    loads += [
        pltpu.make_async_copy(
            err_hbm.at[pl.ds(c * QUART, QUART)], err.at[pl.ds(c * QUART, QUART)], loc.at[3 + c]
        )
        for c in range(4)
    ]
    loads.insert(2, pltpu.make_async_copy(grad_hbm, grad, loc.at[2]))
    for load in loads:
        load.start()

    barrier = pltpu.get_barrier_semaphore()
    pl.semaphore_signal(barrier, 1, device_id=(sibling, z), device_id_type=MESH)
    for d in FAR_XY:
        to = chip_at(d)
        pl.semaphore_signal(barrier, 1, device_id=(to, z), device_id_type=MESH)
        pl.semaphore_signal(barrier, 1, device_id=(to, partner), device_id_type=MESH)
    for d in FAR_Z:
        pl.semaphore_signal(barrier, 1, device_id=(dp, (z + d) % NZ), device_id_type=MESH)

    sends = []

    def finish():
        for fn in sends:
            fn()


    loads[0].wait()
    q_hi, q_lo = split(qt[...])
    q2 = jnp.concatenate([q_hi, q_lo], axis=0)
    loads[1].wait()
    images = sum_terms(dot(hid[...], jnp.concatenate([q2, q2], axis=0), NT))
    img_send[...] = pack(images.reshape(NZ, BLOCK, LANES))
    loads[2].wait()
    pl.semaphore_wait(barrier, 2 * CHIPS + NZ - 2)
    for d in FAR_Z:
        to = (z + d) % NZ
        send(img_send.at[to], img_recv.at[d - 1], img_s, img_r, (dp, to))
    sends.append(lambda: take(img_send.at[pl.ds(0, NZ - 1)], img_s))

    for c in range(4):
        loads[3 + c].wait()
        part = dot(q2, err[pl.ds(c * QUART, QUART), :], NT)
        pt[:, pl.ds(c * QUART, QUART)] = part[:R] + part[R:]
    by_quarter = hid[...].astype(F32).reshape(NZ, 4, 4, F)
    by_quarter = [by_quarter[:, g].reshape(TOK // 4, F) for g in range(4)]
    hidp[...] = jnp.concatenate(by_quarter, axis=0).astype(BF16)

    take(img_recv, img_r)
    im_hi, im_lo = split(unpack(jnp.sum(img_recv[...], axis=0) + img_send[z]))
    im2 = jnp.concatenate([im_hi, im_lo], axis=0)
    for dy in FAR:
        c = (y + dy) % 4
        cols = pl.ds(aligned(c * QUART, LANES), QUART)
        part = dot(im2, grad[:, cols], NN)
        pt[:, cols] += part[:R] + part[R:]
        theirs = pl.ds(aligned(c * QUART + (1 - core) * HALF, LANES), HALF)
        send(pt.at[:, theirs], core_recv.at[c], core_s, core_r.at[c], (sibling, z))
    sends.append(lambda: take(core_recv, core_s))

    for dy in FAR:
        c = (y + dy) % 4
        take(core_recv.at[c], core_r.at[c])
        mine = pt[:, pl.ds(aligned(c * QUART + core * HALF, LANES), HALF)] + core_recv[c]
        for g in range(4):
            rs_send[4 * c + g] = mine[8 * g : 8 * g + 8]
        for dx in FAR:
            t = 4 * c + (x + dx) % 4
            for to, first in ((partner, 1 - odd), (z, odd)):
                if dy or dx or to is partner:
                    src = rs_send.at[t, :, pl.ds(aligned(first * LANES, LANES), 2 * LANES)]
                    send(src, rs_recv.at[2 * chip + odd], rs_s, rs_r, (2 * t + core, to))
    heard = rs_recv.at[pl.ds(0, 2 * CHIPS - 1)]
    sends.append(lambda: take(heard, rs_s))
    mine = pl.ds(aligned(odd * LANES, LANES), 2 * LANES)
    rs_recv[2 * chip + odd] = rs_send[chip, :, mine]
    take(heard, rs_r)

    zrecv[pair] = jnp.sum(rs_recv[...], axis=0)
    for d in FAR_Z:
        if d % 2:
            continue
        send(zrecv.at[pair], zrecv.at[pair], z_s, z_r, (dp, (z + d) % NZ))
    others = zrecv.at[pl.ds(0, NZ // 2 - 1)]
    sends.append(lambda: take(others, z_s))
    take(others, z_r)
    rows = pl.ds(aligned(8 * x, 8), 8)
    base = y * QUART + core * HALF
    sums = jnp.sum(zrecv[...], axis=0) * SCALE
    first_two = ptf.at[rows, pl.ds(aligned(base, LANES), 2 * LANES)]
    last = ptf.at[rows, pl.ds(aligned(base + 2 * LANES, LANES), LANES)]

    def spread(window):
        for d in FAR_XY:
            send(window, window, ag_s, ag_r.at[chip], (chip_at(d), partner))
            send(window, window, ag_s, ag_r.at[chip], (chip_at(d), z))
        send(window, window, ag_s, ag_r.at[chip], (dp, partner))

    @pl.when(odd == 0)
    def _():
        first_two[...] = sums
        spread(first_two)
        take(last, ag_r.at[chip])

    @pl.when(odd == 1)
    def _():
        last[...] = sums[:, LANES:]
        spread(last)
        take(first_two, ag_r.at[chip])

    def spread_sends():
        @pl.when(odd == 0)
        def _():
            take(heard, ag_s)

        @pl.when(odd == 1)
        def _():
            take(rs_recv.at[pl.ds(0, 2 * CHIPS - 1), :, pl.ds(0, LANES)], ag_s)

    sends.append(spread_sends)
    for dy in range(4):
        yy = (y + dy) % 4
        for dx in range(1 if dy == 0 else 0, 4):
            xx = (x + dx) % 4
            there = ptf.at[
                pl.ds(aligned(8 * xx, 8), 8), pl.ds(aligned(yy * QUART + core * HALF, LANES), HALF)
            ]
            take(there, ag_r.at[4 * yy + xx])
        block = ptf.at[:, pl.ds(aligned(yy * QUART + core * HALF, LANES), HALF)]
        send(block, block, fwd_s, fwd_r, (sibling, z))
    sends.append(lambda: take(core_recv, fwd_s))
    take(core_recv, fwd_r)

    p_hi, p_lo = split(ptf[...])
    p2 = jnp.concatenate([p_hi, p_lo], axis=0)
    w = dot(grad[...], jnp.concatenate([p2, p2], axis=0), NT)
    wrecv[z] = pack(sum_terms(w))
    for d in FAR_Z:
        send(wrecv.at[z], wrecv.at[z], w_s, w_r, (dp, (z + d) % NZ))
    far = wrecv.at[pl.ds(0, NZ - 1)]
    sends.append(lambda: take(far, w_s))

    part = dot(p2, err[...], NN)
    s_err = part[:R] + part[R:]
    gram = dot(p2, p2, NT)
    gram = gram[:R, :R] + gram[R:, R:] + (gram[:R, R:] + gram[R:, :R])

    linv[...] = inverse_factor(gram)
    first = aligned((3 * z) // 2 * LANES, LANES)
    mid = ptf[:, pl.ds(first, 2 * LANES)]
    mid = jnp.where(z % 2 == 1, mid[:, 64:], mid[:, :192])
    basis_ref[...] = jnp.dot(linv[...], mid, precision=HIGH, preferred_element_type=F32) * (
        float(D) ** 0.5
    )

    take(far, w_r)
    w_hi, w_lo = split(unpack(wrecv[...].reshape(TOK // 4, LANES)))
    part = dot(jnp.concatenate([w_hi, w_lo], axis=0), hidp[...], NN)
    s_buf[...] = s_err + part[:R] + part[R:]

    my_cols = pl.ds(aligned(core * HALF, LANES), HALF)
    their_cols = pl.ds(aligned((1 - core) * HALF, LANES), HALF)
    send(s_buf.at[:, their_cols], s_core, sc_s, sc_r, (sibling, z))
    sends.append(lambda: take(s_core, sc_s))
    take(s_core, sc_r)
    mine = s_buf[:, my_cols] + s_core[...]

    def exchange(along_x, along_y, sx_s, sx_r, sy_s, sy_r):
        for d in range(1, 4):
            to = 2 * (4 * y + (x + d) % 4) + core
            send(along_x.at[x], along_x.at[x], sx_s, sx_r, (to, z))
            to = 2 * (4 * ((y + d) % 4) + x) + core
            send(along_y.at[y], along_y.at[y], sy_s, sy_r, (to, z))
        sends.append(lambda: take(along_x.at[pl.ds(0, 3)], sx_s))
        sends.append(lambda: take(along_y.at[pl.ds(0, 3)], sy_s))

    sx[x] = mine[: R // 2]
    sy[y] = mine[R // 2 :]
    exchange(sx, sy, sx_s, sx_r, sy_s, sy_r)

    take(sx.at[pl.ds(0, 3)], sx_r)
    take(sy.at[pl.ds(0, 3)], sy_r)
    sy2[y] = jnp.sum(sx[...], axis=0)
    sx2[x] = jnp.sum(sy[...], axis=0)
    exchange(sx2, sy2, sx2_s, sx2_r, sy2_s, sy2_r)
    take(sx2.at[pl.ds(0, 3)], sx2_r)
    take(sy2.at[pl.ds(0, 3)], sy2_r)
    s = jnp.concatenate([jnp.sum(sy2[...], axis=0), jnp.sum(sx2[...], axis=0)], axis=0)
    my_q = qnew_ref.at[:, my_cols]
    my_q[...] = jnp.dot(linv[...], s, precision=HIGH, preferred_element_type=F32) * (1.0 / DP)
    send(my_q, my_q, q_s, q_r, (sibling, z))
    sends.append(lambda: take(s_core, q_s))
    take(qnew_ref.at[:, their_cols], q_r)
    finish()


def body(grad_out, hidden, error, q_init):
    one, many = pltpu.SemaphoreType.DMA, lambda n: pltpu.SemaphoreType.DMA((n,))
    vmem = pltpu.VMEM
    basis, q_new = pl.pallas_call(
        kernel,
        out_shape=(pltpu.VMEM((R, D // NZ), F32), pltpu.VMEM((R, F), F32)),
        in_specs=[pl.BlockSpec(memory_space=pltpu.HBM)] * 4,
        out_specs=[pl.BlockSpec(memory_space=pltpu.VMEM)] * 2,
        scratch_shapes=[
            vmem((BLOCK, D), BF16),
            vmem((TOK, F), BF16),
            vmem((D, F), BF16),
            vmem((R, F), F32),
            vmem((TOK, F), BF16),
            vmem((R, D), F32),
            vmem((NZ, 4, LANES), F32),
            vmem((NZ - 1, 4, LANES), F32),
            vmem((4, R, HALF), F32),
            vmem((CHIPS, 8, HALF), F32),
            vmem((2 * CHIPS, 8, 2 * LANES), F32),
            vmem((NZ // 2, 8, 2 * LANES), F32),
            vmem((R, D), F32),
            vmem((NZ, 4, LANES), F32),
            vmem((R, F), F32),
            vmem((R, HALF), F32),
            vmem((4, R // 2, HALF), F32),
            vmem((4, R // 2, HALF), F32),
            vmem((4, R // 2, HALF), F32),
            vmem((4, R // 2, HALF), F32),
            vmem((R, R), F32),
            many(7),
            one, one,
            one, many(4),
            one, one,
            one, one,
            one, many(CHIPS),
            one, one,
            one, one,
            one, one,
            one, one,
            one, one,
            one, one,
            one, one,
            one, one,
        ],
        compiler_params=pltpu.CompilerParams(
            collective_id=0, has_side_effects=True, vmem_limit_bytes=60 * 1024 * 1024
        ),
    )(grad_out[0], hidden[0], error[0], q_init.T)
    return basis.T, q_new.T


def solution(mesh):
    return jax.shard_map(
        body,
        mesh=mesh,
        in_specs=(
            P("dp", "tensor", None),
            P("dp", None, "tensor"),
            P("dp", None, "tensor"),
            P("tensor", None),
        ),
        out_specs=(P("tensor", None), P("tensor", None)),
        check_vma=False,
    )
```

```python
import functools

import jax
import jax.numpy as jnp
from jax import lax
from jax.experimental import pallas as pl
from jax.experimental.pallas import tpu as pltpu
from jax.sharding import PartitionSpec as P

MESH = pl.DeviceIdType.MESH
NT = (((1,), (1,)), ((), ()))
NN = (((1,), (0,)), ((), ()))
F32, BF16 = jnp.float32, jnp.bfloat16
HIGH = lax.Precision.HIGHEST

NZ, CHIPS, DP = 16, 16, 32
D, F, R, TOK = 3072, 768, 32, 256
LANES, HALF, QUART = 128, 384, 768
FAR = (2, 1, 3, 0)
FAR_Z = sorted(range(1, NZ), key=lambda d: -min(d, NZ - d))
FAR_XY = sorted(range(1, CHIPS), key=lambda d: -min(d % 4, 4 - d % 4) - min(d // 4, 4 - d // 4))
SCALE = 2.0**20
BLOCK = TOK // NZ


def dot(a, b, dims):
    return lax.dot_general(a, b, dims, preferred_element_type=F32)


def split(v):
    hi = v.astype(BF16)
    return hi, (v - hi.astype(F32)).astype(BF16)


def take(ref, sem):
    pltpu.make_async_copy(ref, ref, sem).wait()


def aligned(i, n):
    return pl.multiple_of(i, n)


def sum_terms(v):
    return v + pltpu.roll(v, R, 1)


def pack(v):
    quarter = lax.broadcasted_iota(jnp.int32, (1, LANES), 1) // R
    v = jnp.where(quarter < 2, v[..., :8, :], v[..., 8:, :])
    return jnp.where(quarter % 2 == 0, v[..., :4, :], v[..., 4:, :])


def unpack(v):
    v = v.T
    return jnp.concatenate([v[R * g : R * g + R] for g in range(4)], axis=1)


def inverse_factor(gram):
    row = lax.broadcasted_iota(jnp.int32, (R, 2 * R), 0)
    col = lax.broadcasted_iota(jnp.int32, (R, 2 * R), 1)
    one = (col - R == row).astype(F32)
    a = jnp.concatenate([gram, one[:, R:]], axis=1)
    for k in range(R):
        pivot = a[k : k + 1, :]
        step = jnp.where(row[:, :1] > k, a[:, k : k + 1] / a[k : k + 1, k : k + 1], 0.0)
        a = a - step * pivot
    diag = jnp.sum(jnp.where(row == col, a, 0.0), axis=1, keepdims=True)
    return a[:, R:] / jnp.sqrt(diag)


def kernel(
    grad_hbm, hid_hbm, err_hbm, qt_hbm, basis_ref, qnew_ref,
    grad, hid, err, qt, hidp, pt, img_send, img_recv, core_recv, rs_send, rs_recv,
    zrecv, ptf, wrecv, s_buf, s_core, sx, sy, sx2, sy2, linv,
    loc, img_s, img_r, core_s, core_r, rs_s, rs_r, z_s, z_r,
    ag_s, ag_r, fwd_s, fwd_r, w_s, w_r, sc_s, sc_r, sx_s, sx_r, sy_s, sy_r,
    sx2_s, sx2_r, sy2_s, sy2_r,
):
    dp = lax.axis_index("dp")
    z = lax.axis_index("tensor")
    core, chip = dp % 2, dp // 2
    x, y = chip % 4, chip // 4
    sibling = dp + 1 - 2 * core
    odd, pair = z % 2, z // 2
    partner = z + 1 - 2 * odd

    def chip_at(d):
        return 2 * (4 * ((y + d // 4) % 4) + (x + d % 4) % 4) + core

    def send(src, dst, s, r, to):
        copy = pltpu.make_async_remote_copy(
            src_ref=src, dst_ref=dst, send_sem=s, recv_sem=r,
            device_id=to, device_id_type=MESH,
        )
        copy.start()

    barrier = pltpu.get_barrier_semaphore()
    for d in FAR_Z:
        pl.semaphore_signal(barrier, 1, device_id=(dp, (z + d) % NZ), device_id_type=MESH)
    pl.semaphore_signal(barrier, 1, device_id=(sibling, z), device_id_type=MESH)
    for d in FAR[:3]:
        for to in (chip_at(d), chip_at(4 * d)):
            to = to + 1 - 2 * core
            pl.semaphore_signal(barrier, 1, device_id=(to, z), device_id_type=MESH)
    for d in FAR_XY:
        to = chip_at(d)
        pl.semaphore_signal(barrier, 1, device_id=(to, z), device_id_type=MESH)
        pl.semaphore_signal(barrier, 1, device_id=(to, partner), device_id_type=MESH)

    loads = [
        pltpu.make_async_copy(qt_hbm, qt, loc.at[0]),
        pltpu.make_async_copy(hid_hbm, hid, loc.at[1]),
    ]
    loads += [
        pltpu.make_async_copy(
            err_hbm.at[pl.ds(c * QUART, QUART)], err.at[pl.ds(c * QUART, QUART)], loc.at[3 + c]
        )
        for c in range(4)
    ]
    loads.insert(2, pltpu.make_async_copy(grad_hbm, grad, loc.at[2]))
    for load in loads:
        load.start()

    sends = []

    def finish():
        for fn in sends:
            fn()


    loads[0].wait()
    q_hi, q_lo = split(qt[...])
    q2 = jnp.concatenate([q_hi, q_lo], axis=0)
    loads[1].wait()
    images = sum_terms(dot(hid[...], jnp.concatenate([q2, q2], axis=0), NT))
    img_send[...] = pack(images.reshape(NZ, BLOCK, LANES))
    loads[2].wait()
    pl.semaphore_wait(barrier, 2 * CHIPS + NZ + 4)
    for d in FAR_Z:
        to = (z + d) % NZ
        send(img_send.at[to], img_recv.at[d - 1], img_s, img_r, (dp, to))
    sends.append(lambda: take(img_send.at[pl.ds(0, NZ - 1)], img_s))

    for c in range(4):
        loads[3 + c].wait()
        part = dot(q2, err[pl.ds(c * QUART, QUART), :], NT)
        pt[:, pl.ds(c * QUART, QUART)] = part[:R] + part[R:]
    by_quarter = hid[...].astype(F32).reshape(NZ, 4, 4, F)
    by_quarter = [by_quarter[:, g].reshape(TOK // 4, F) for g in range(4)]
    hidp[...] = jnp.concatenate(by_quarter, axis=0).astype(BF16)

    take(img_recv, img_r)
    im_hi, im_lo = split(unpack(jnp.sum(img_recv[...], axis=0) + img_send[z]))
    im2 = jnp.concatenate([im_hi, im_lo], axis=0)
    for dy in FAR:
        c = (y + dy) % 4
        cols = pl.ds(aligned(c * QUART, LANES), QUART)
        part = dot(im2, grad[:, cols], NN)
        pt[:, cols] += part[:R] + part[R:]
        theirs = pl.ds(aligned(c * QUART + (1 - core) * HALF, LANES), HALF)
        send(pt.at[:, theirs], core_recv.at[c], core_s, core_r.at[c], (sibling, z))
    sends.append(lambda: take(core_recv, core_s))

    for dy in FAR:
        c = (y + dy) % 4
        take(core_recv.at[c], core_r.at[c])
        mine = pt[:, pl.ds(aligned(c * QUART + core * HALF, LANES), HALF)] + core_recv[c]
        for g in range(4):
            rs_send[4 * c + g] = mine[8 * g : 8 * g + 8]
        for dx in FAR:
            t = 4 * c + (x + dx) % 4
            for to, first in ((partner, 1 - odd), (z, odd)):
                if dy or dx or to is partner:
                    src = rs_send.at[t, :, pl.ds(aligned(first * LANES, LANES), 2 * LANES)]
                    send(src, rs_recv.at[2 * chip + odd], rs_s, rs_r, (2 * t + core, to))
    heard = rs_recv.at[pl.ds(0, 2 * CHIPS - 1)]
    sends.append(lambda: take(heard, rs_s))
    mine = pl.ds(aligned(odd * LANES, LANES), 2 * LANES)
    rs_recv[2 * chip + odd] = rs_send[chip, :, mine]
    take(heard, rs_r)

    zrecv[pair] = jnp.sum(rs_recv[...], axis=0)
    for d in FAR_Z:
        if d % 2:
            continue
        send(zrecv.at[pair], zrecv.at[pair], z_s, z_r, (dp, (z + d) % NZ))
    others = zrecv.at[pl.ds(0, NZ // 2 - 1)]
    sends.append(lambda: take(others, z_s))
    take(others, z_r)
    rows = pl.ds(aligned(8 * x, 8), 8)
    base = y * QUART + core * HALF
    sums = jnp.sum(zrecv[...], axis=0) * SCALE
    first_two = ptf.at[rows, pl.ds(aligned(base, LANES), 2 * LANES)]
    last = ptf.at[rows, pl.ds(aligned(base + 2 * LANES, LANES), LANES)]

    def spread(window):
        for d in FAR_XY:
            send(window, window, ag_s, ag_r.at[chip], (chip_at(d), partner))
            send(window, window, ag_s, ag_r.at[chip], (chip_at(d), z))
        send(window, window, ag_s, ag_r.at[chip], (dp, partner))

    @pl.when(odd == 0)
    def _():
        first_two[...] = sums
        spread(first_two)
        take(last, ag_r.at[chip])

    @pl.when(odd == 1)
    def _():
        last[...] = sums[:, LANES:]
        spread(last)
        take(first_two, ag_r.at[chip])

    def spread_sends():
        @pl.when(odd == 0)
        def _():
            take(heard, ag_s)

        @pl.when(odd == 1)
        def _():
            take(rs_recv.at[pl.ds(0, 2 * CHIPS - 1), :, pl.ds(0, LANES)], ag_s)

    sends.append(spread_sends)
    for dy in range(4):
        yy = (y + dy) % 4
        for dx in range(1 if dy == 0 else 0, 4):
            xx = (x + dx) % 4
            there = ptf.at[
                pl.ds(aligned(8 * xx, 8), 8), pl.ds(aligned(yy * QUART + core * HALF, LANES), HALF)
            ]
            take(there, ag_r.at[4 * yy + xx])
        block = ptf.at[:, pl.ds(aligned(yy * QUART + core * HALF, LANES), HALF)]
        send(block, block, fwd_s, fwd_r, (sibling, z))
    sends.append(lambda: take(core_recv, fwd_s))
    take(core_recv, fwd_r)

    p_hi, p_lo = split(ptf[...])
    p2 = jnp.concatenate([p_hi, p_lo], axis=0)
    w = dot(grad[...], jnp.concatenate([p2, p2], axis=0), NT)
    wrecv[z] = pack(sum_terms(w))
    for d in FAR_Z:
        send(wrecv.at[z], wrecv.at[z], w_s, w_r, (dp, (z + d) % NZ))
    far = wrecv.at[pl.ds(0, NZ - 1)]
    sends.append(lambda: take(far, w_s))

    part = dot(p2, err[...], NN)
    s_err = part[:R] + part[R:]
    gram = dot(p2, p2, NT)
    gram = gram[:R, :R] + gram[R:, R:] + (gram[:R, R:] + gram[R:, :R])

    linv[...] = inverse_factor(gram)
    first = aligned((3 * z) // 2 * LANES, LANES)
    mid = ptf[:, pl.ds(first, 2 * LANES)]
    mid = jnp.where(z % 2 == 1, mid[:, 64:], mid[:, :192])
    basis_ref[...] = jnp.dot(linv[...], mid, precision=HIGH, preferred_element_type=F32) * (
        float(D) ** 0.5
    )

    take(far, w_r)
    w_hi, w_lo = split(unpack(wrecv[...].reshape(TOK // 4, LANES)))
    part = dot(jnp.concatenate([w_hi, w_lo], axis=0), hidp[...], NN)
    s_buf[...] = s_err + part[:R] + part[R:]

    my_cols = pl.ds(aligned(core * HALF, LANES), HALF)
    their_cols = pl.ds(aligned((1 - core) * HALF, LANES), HALF)
    send(s_buf.at[:, their_cols], s_core, sc_s, sc_r, (sibling, z))
    sends.append(lambda: take(s_core, sc_s))
    take(s_core, sc_r)
    mine = s_buf[:, my_cols] + s_core[...]

    def exchange(along_x, at_x, along_y, at_y, sems, both):
        sx_s, sx_r, sy_s, sy_r = sems
        x_block, y_block = along_x.at[at_x], along_y.at[at_y]
        for d in FAR if both else FAR[:3]:
            for to, block, s, r in (
                (chip_at(d), x_block, sx_s, sx_r),
                (chip_at(4 * d), y_block, sy_s, sy_r),
            ):
                if d:
                    send(block, block, s, r, (to, z))
                if both:
                    send(block, block, s, r, (to + 1 - 2 * core, z))
        n = 7 if both else 3
        sends.append(lambda: take(along_x.at[pl.ds(0, n)], sx_s))
        sends.append(lambda: take(along_y.at[pl.ds(0, n)], sy_s))

    sx[x] = mine[: R // 2]
    sy[y] = mine[R // 2 :]
    exchange(sx, x, sy, y, (sx_s, sx_r, sy_s, sy_r), False)

    take(sx.at[pl.ds(0, 3)], sx_r)
    take(sy.at[pl.ds(0, 3)], sy_r)
    at_x, at_y = 4 * core + x, 4 * core + y
    sy2[at_y] = jnp.sum(sx[...], axis=0)
    sx2[at_x] = jnp.sum(sy[...], axis=0)
    exchange(sx2, at_x, sy2, at_y, (sx2_s, sx2_r, sy2_s, sy2_r), True)
    take(sx2.at[pl.ds(0, 7)], sx2_r)
    take(sy2.at[pl.ds(0, 7)], sy2_r)
    for half in range(2):
        part = [jnp.sum(v[4 * half : 4 * half + 4], axis=0) for v in (sy2, sx2)]
        part = jnp.dot(
            linv[...], jnp.concatenate(part, axis=0), precision=HIGH, preferred_element_type=F32
        )
        qnew_ref[:, half * HALF : (half + 1) * HALF] = part * (1.0 / DP)
    finish()


def body(grad_out, hidden, error, q_init):
    one, many = pltpu.SemaphoreType.DMA, lambda n: pltpu.SemaphoreType.DMA((n,))
    vmem = pltpu.VMEM
    basis, q_new = pl.pallas_call(
        kernel,
        out_shape=(pltpu.VMEM((R, D // NZ), F32), pltpu.VMEM((R, F), F32)),
        in_specs=[pl.BlockSpec(memory_space=pltpu.HBM)] * 4,
        out_specs=[pl.BlockSpec(memory_space=pltpu.VMEM)] * 2,
        scratch_shapes=[
            vmem((BLOCK, D), BF16),
            vmem((TOK, F), BF16),
            vmem((D, F), BF16),
            vmem((R, F), F32),
            vmem((TOK, F), BF16),
            vmem((R, D), F32),
            vmem((NZ, 4, LANES), F32),
            vmem((NZ - 1, 4, LANES), F32),
            vmem((4, R, HALF), F32),
            vmem((CHIPS, 8, HALF), F32),
            vmem((2 * CHIPS, 8, 2 * LANES), F32),
            vmem((NZ // 2, 8, 2 * LANES), F32),
            vmem((R, D), F32),
            vmem((NZ, 4, LANES), F32),
            vmem((R, F), F32),
            vmem((R, HALF), F32),
            vmem((4, R // 2, HALF), F32),
            vmem((4, R // 2, HALF), F32),
            vmem((8, R // 2, HALF), F32),
            vmem((8, R // 2, HALF), F32),
            vmem((R, R), F32),
            many(7),
            one, one,
            one, many(4),
            one, one,
            one, one,
            one, many(CHIPS),
            one, one,
            one, one,
            one, one,
            one, one,
            one, one,
            one, one,
            one, one,
        ],
        compiler_params=pltpu.CompilerParams(
            collective_id=0, has_side_effects=True, vmem_limit_bytes=60 * 1024 * 1024
        ),
    )(grad_out[0], hidden[0], error[0], q_init.T)
    return basis.T, q_new.T


def solution(mesh):
    return jax.shard_map(
        body,
        mesh=mesh,
        in_specs=(
            P("dp", "tensor", None),
            P("dp", None, "tensor"),
            P("dp", None, "tensor"),
            P("tensor", None),
        ),
        out_specs=(P("tensor", None), P("tensor", None)),
        check_vma=False,
    )
```

```python
import functools

import jax
import jax.numpy as jnp
from jax import lax
from jax.experimental import pallas as pl
from jax.experimental.pallas import tpu as pltpu
from jax.sharding import PartitionSpec as P

MESH = pl.DeviceIdType.MESH
NT = (((1,), (1,)), ((), ()))
NN = (((1,), (0,)), ((), ()))
F32, BF16 = jnp.float32, jnp.bfloat16
HIGH = lax.Precision.HIGHEST

NZ, CHIPS, DP = 16, 16, 32
D, F, R, TOK = 3072, 768, 32, 256
LANES, HALF, QUART = 128, 384, 768
FAR = (2, 1, 3, 0)
FAR_Z = sorted(range(1, NZ), key=lambda d: -min(d, NZ - d))
FAR_XY = sorted(range(1, CHIPS), key=lambda d: -min(d % 4, 4 - d % 4) - min(d // 4, 4 - d // 4))
SCALE = 2.0**20
BLOCK = TOK // NZ


def dot(a, b, dims):
    return lax.dot_general(a, b, dims, preferred_element_type=F32)


def split(v):
    hi = v.astype(BF16)
    return hi, (v - hi.astype(F32)).astype(BF16)


def take(ref, sem):
    pltpu.make_async_copy(ref, ref, sem).wait()


def aligned(i, n):
    return pl.multiple_of(i, n)


def sum_terms(v):
    return v + pltpu.roll(v, R, 1)


def pack(v):
    quarter = lax.broadcasted_iota(jnp.int32, (1, LANES), 1) // R
    v = jnp.where(quarter < 2, v[..., :8, :], v[..., 8:, :])
    return jnp.where(quarter % 2 == 0, v[..., :4, :], v[..., 4:, :])


def unpack(v):
    v = v.T
    return jnp.concatenate([v[R * g : R * g + R] for g in range(4)], axis=1)


def inverse_factor(gram):
    row = lax.broadcasted_iota(jnp.int32, (R, 2 * R), 0)
    col = lax.broadcasted_iota(jnp.int32, (R, 2 * R), 1)
    one = (col - R == row).astype(F32)
    a = jnp.concatenate([gram, one[:, R:]], axis=1)
    for k in range(R):
        pivot = a[k : k + 1, :]
        step = jnp.where(row[:, :1] > k, a[:, k : k + 1] / a[k : k + 1, k : k + 1], 0.0)
        a = a - step * pivot
    diag = jnp.sum(jnp.where(row == col, a, 0.0), axis=1, keepdims=True)
    return a[:, R:] / jnp.sqrt(diag)


def kernel(
    grad_hbm, hid_hbm, err_hbm, qt_hbm, basis_ref, qnew_ref,
    grad, hid, err, qt, hidp, pt, img_send, img_recv, core_recv, rs_send, rs_recv,
    zrecv, ptf, wrecv, s_buf, s_core, sx, sy, sx2, sy2, linv,
    loc, img_s, img_r, core_s, core_r, rs_s, rs_r, z_s, z_r,
    ag_s, ag_r, fwd_s, fwd_r, w_s, w_r, sc_s, sc_r, sx_s, sx_r, sy_s, sy_r,
    sx2_s, sx2_r, sy2_s, sy2_r,
):
    dp = lax.axis_index("dp")
    z = lax.axis_index("tensor")
    core, chip = dp % 2, dp // 2
    x, y = chip % 4, chip // 4
    sibling = dp + 1 - 2 * core
    odd, pair = z % 2, z // 2
    partner = z + 1 - 2 * odd

    def chip_at(d):
        return 2 * (4 * ((y + d // 4) % 4) + (x + d % 4) % 4) + core

    def send(src, dst, s, r, to):
        copy = pltpu.make_async_remote_copy(
            src_ref=src, dst_ref=dst, send_sem=s, recv_sem=r,
            device_id=to, device_id_type=MESH,
        )
        copy.start()

    barrier = pltpu.get_barrier_semaphore()
    for d in FAR_Z:
        pl.semaphore_signal(barrier, 1, device_id=(dp, (z + d) % NZ), device_id_type=MESH)
    pl.semaphore_signal(barrier, 1, device_id=(sibling, z), device_id_type=MESH)
    for d in FAR[:3]:
        for to in (chip_at(d), chip_at(4 * d)):
            to = to + 1 - 2 * core
            pl.semaphore_signal(barrier, 1, device_id=(to, z), device_id_type=MESH)
    for d in FAR_XY:
        to = chip_at(d)
        pl.semaphore_signal(barrier, 1, device_id=(to, z), device_id_type=MESH)
        pl.semaphore_signal(barrier, 1, device_id=(to, partner), device_id_type=MESH)

    loads = [
        pltpu.make_async_copy(qt_hbm, qt, loc.at[0]),
        pltpu.make_async_copy(hid_hbm, hid, loc.at[1]),
    ]
    loads += [
        pltpu.make_async_copy(
            err_hbm.at[pl.ds(c * QUART, QUART)], err.at[pl.ds(c * QUART, QUART)], loc.at[3 + c]
        )
        for c in range(4)
    ]
    loads.insert(2, pltpu.make_async_copy(grad_hbm, grad, loc.at[2]))
    for load in loads:
        load.start()

    sends = []

    def finish():
        for fn in sends:
            fn()
        sends.clear()


    loads[0].wait()
    q_hi, q_lo = split(qt[...])
    q2 = jnp.concatenate([q_hi, q_lo], axis=0)
    loads[1].wait()
    images = sum_terms(dot(hid[...], jnp.concatenate([q2, q2], axis=0), NT))
    img_send[...] = pack(images.reshape(NZ, BLOCK, LANES))
    loads[2].wait()
    pl.semaphore_wait(barrier, 2 * CHIPS + NZ + 4)
    for d in FAR_Z:
        to = (z + d) % NZ
        send(img_send.at[to], img_recv.at[d - 1], img_s, img_r, (dp, to))
    sends.append(lambda: take(img_send.at[pl.ds(0, NZ - 1)], img_s))

    for c in range(4):
        loads[3 + c].wait()
        part = dot(q2, err[pl.ds(c * QUART, QUART), :], NT)
        pt[:, pl.ds(c * QUART, QUART)] = part[:R] + part[R:]
    by_quarter = hid[...].astype(F32).reshape(NZ, 4, 4, F)
    by_quarter = [by_quarter[:, g].reshape(TOK // 4, F) for g in range(4)]
    hidp[...] = jnp.concatenate(by_quarter, axis=0).astype(BF16)

    take(img_recv, img_r)
    im_hi, im_lo = split(unpack(jnp.sum(img_recv[...], axis=0) + img_send[z]))
    im2 = jnp.concatenate([im_hi, im_lo], axis=0)
    for dy in FAR:
        c = (y + dy) % 4
        cols = pl.ds(aligned(c * QUART, LANES), QUART)
        part = dot(im2, grad[:, cols], NN)
        pt[:, cols] += part[:R] + part[R:]
        theirs = pl.ds(aligned(c * QUART + (1 - core) * HALF, LANES), HALF)
        send(pt.at[:, theirs], core_recv.at[c], core_s, core_r.at[c], (sibling, z))
    sends.append(lambda: take(core_recv, core_s))

    for dy in FAR:
        c = (y + dy) % 4
        take(core_recv.at[c], core_r.at[c])
        mine = pt[:, pl.ds(aligned(c * QUART + core * HALF, LANES), HALF)] + core_recv[c]
        for g in range(4):
            rs_send[4 * c + g] = mine[8 * g : 8 * g + 8]
        for dx in FAR:
            t = 4 * c + (x + dx) % 4
            for to, first in ((partner, 1 - odd), (z, odd)):
                if dy or dx or to is partner:
                    src = rs_send.at[t, :, pl.ds(aligned(first * LANES, LANES), 2 * LANES)]
                    send(src, rs_recv.at[2 * chip + odd], rs_s, rs_r, (2 * t + core, to))
    heard = rs_recv.at[pl.ds(0, 2 * CHIPS - 1)]
    sends.append(lambda: take(heard, rs_s))
    mine = pl.ds(aligned(odd * LANES, LANES), 2 * LANES)
    rs_recv[2 * chip + odd] = rs_send[chip, :, mine]
    take(heard, rs_r)

    zrecv[pair] = jnp.sum(rs_recv[...], axis=0)
    for d in FAR_Z:
        if d % 2:
            continue
        send(zrecv.at[pair], zrecv.at[pair], z_s, z_r, (dp, (z + d) % NZ))
    others = zrecv.at[pl.ds(0, NZ // 2 - 1)]
    sends.append(lambda: take(others, z_s))
    take(others, z_r)
    rows = pl.ds(aligned(8 * x, 8), 8)
    base = y * QUART + core * HALF
    sums = jnp.sum(zrecv[...], axis=0) * SCALE
    first_two = ptf.at[rows, pl.ds(aligned(base, LANES), 2 * LANES)]
    last = ptf.at[rows, pl.ds(aligned(base + 2 * LANES, LANES), LANES)]

    def spread(window):
        for d in FAR_XY:
            send(window, window, ag_s, ag_r.at[chip], (chip_at(d), partner))
            send(window, window, ag_s, ag_r.at[chip], (chip_at(d), z))
        send(window, window, ag_s, ag_r.at[chip], (dp, partner))

    @pl.when(odd == 0)
    def _():
        first_two[...] = sums
        spread(first_two)
        take(last, ag_r.at[chip])

    @pl.when(odd == 1)
    def _():
        last[...] = sums[:, LANES:]
        spread(last)
        take(first_two, ag_r.at[chip])

    def spread_sends():
        @pl.when(odd == 0)
        def _():
            take(heard, ag_s)

        @pl.when(odd == 1)
        def _():
            take(rs_recv.at[pl.ds(0, 2 * CHIPS - 1), :, pl.ds(0, LANES)], ag_s)

    sends.append(spread_sends)
    for d in [0] + FAR_XY[::-1]:
        yy, xx = (y + d // 4) % 4, (x + d % 4) % 4
        there = ptf.at[
            pl.ds(aligned(8 * xx, 8), 8), pl.ds(aligned(yy * QUART + core * HALF, LANES), HALF)
        ]
        if d:
            take(there, ag_r.at[4 * yy + xx])
        send(there, there, fwd_s, fwd_r, (sibling, z))
    sends.append(lambda: take(core_recv, fwd_s))
    take(core_recv, fwd_r)

    p_hi, p_lo = split(ptf[...])
    p2 = jnp.concatenate([p_hi, p_lo], axis=0)
    w = dot(grad[...], jnp.concatenate([p2, p2], axis=0), NT)
    wrecv[z] = pack(sum_terms(w))
    for d in FAR_Z:
        send(wrecv.at[z], wrecv.at[z], w_s, w_r, (dp, (z + d) % NZ))
    finish()
    far = wrecv.at[pl.ds(0, NZ - 1)]
    sends.append(lambda: take(far, w_s))

    part = dot(p2, err[...], NN)
    s_buf[...] = part[:R] + part[R:]
    gram = dot(p2, p2, NT)
    gram = gram[:R, :R] + gram[R:, R:] + (gram[:R, R:] + gram[R:, :R])

    linv[...] = inverse_factor(gram)
    first = aligned((3 * z) // 2 * LANES, LANES)
    mid = ptf[:, pl.ds(first, 2 * LANES)]
    mid = jnp.where(z % 2 == 1, mid[:, 64:], mid[:, :192])
    basis_ref[...] = jnp.dot(linv[...], mid, precision=HIGH, preferred_element_type=F32) * (
        float(D) ** 0.5
    )

    take(far, w_r)
    w_hi, w_lo = split(unpack(wrecv[...].reshape(TOK // 4, LANES)))
    w2 = jnp.concatenate([w_hi, w_lo], axis=0)

    my_cols = pl.ds(aligned(core * HALF, LANES), HALF)
    their_cols = pl.ds(aligned((1 - core) * HALF, LANES), HALF)
    part = dot(w2, hidp[:, their_cols], NN)
    s_buf[:, their_cols] += part[:R] + part[R:]
    send(s_buf.at[:, their_cols], s_core, sc_s, sc_r, (sibling, z))
    part = dot(w2, hidp[:, my_cols], NN)
    s_buf[:, my_cols] += part[:R] + part[R:]
    sends.append(lambda: take(s_core, sc_s))
    take(s_core, sc_r)
    mine = s_buf[:, my_cols] + s_core[...]

    def exchange(along_x, at_x, along_y, at_y, sems, both):
        sx_s, sx_r, sy_s, sy_r = sems
        x_block, y_block = along_x.at[at_x], along_y.at[at_y]
        for d in FAR if both else FAR[:3]:
            for to, block, s, r in (
                (chip_at(d), x_block, sx_s, sx_r),
                (chip_at(4 * d), y_block, sy_s, sy_r),
            ):
                if d:
                    send(block, block, s, r, (to, z))
                if both:
                    send(block, block, s, r, (to + 1 - 2 * core, z))
        n = 7 if both else 3
        sends.append(lambda: take(along_x.at[pl.ds(0, n)], sx_s))
        sends.append(lambda: take(along_y.at[pl.ds(0, n)], sy_s))

    sx[x] = mine[: R // 2]
    sy[y] = mine[R // 2 :]
    exchange(sx, x, sy, y, (sx_s, sx_r, sy_s, sy_r), False)

    take(sx.at[pl.ds(0, 3)], sx_r)
    take(sy.at[pl.ds(0, 3)], sy_r)
    at_x, at_y = 4 * core + x, 4 * core + y
    sy2[at_y] = jnp.sum(sx[...], axis=0)
    sx2[at_x] = jnp.sum(sy[...], axis=0)
    early, sends[:] = list(sends), []
    exchange(sx2, at_x, sy2, at_y, (sx2_s, sx2_r, sy2_s, sy2_r), True)
    for fn in early:
        fn()
    take(sx2.at[pl.ds(0, 7)], sx2_r)
    take(sy2.at[pl.ds(0, 7)], sy2_r)
    for half in range(2):
        part = [jnp.sum(v[4 * half : 4 * half + 4], axis=0) for v in (sy2, sx2)]
        part = jnp.dot(
            linv[...], jnp.concatenate(part, axis=0), precision=HIGH, preferred_element_type=F32
        )
        qnew_ref[:, half * HALF : (half + 1) * HALF] = part * (1.0 / DP)
    finish()


def body(grad_out, hidden, error, q_init):
    one, many = pltpu.SemaphoreType.DMA, lambda n: pltpu.SemaphoreType.DMA((n,))
    vmem = pltpu.VMEM
    basis, q_new = pl.pallas_call(
        kernel,
        out_shape=(pltpu.VMEM((R, D // NZ), F32), pltpu.VMEM((R, F), F32)),
        in_specs=[pl.BlockSpec(memory_space=pltpu.HBM)] * 4,
        out_specs=[pl.BlockSpec(memory_space=pltpu.VMEM)] * 2,
        scratch_shapes=[
            vmem((BLOCK, D), BF16),
            vmem((TOK, F), BF16),
            vmem((D, F), BF16),
            vmem((R, F), F32),
            vmem((TOK, F), BF16),
            vmem((R, D), F32),
            vmem((NZ, 4, LANES), F32),
            vmem((NZ - 1, 4, LANES), F32),
            vmem((4, R, HALF), F32),
            vmem((CHIPS, 8, HALF), F32),
            vmem((2 * CHIPS, 8, 2 * LANES), F32),
            vmem((NZ // 2, 8, 2 * LANES), F32),
            vmem((R, D), F32),
            vmem((NZ, 4, LANES), F32),
            vmem((R, F), F32),
            vmem((R, HALF), F32),
            vmem((4, R // 2, HALF), F32),
            vmem((4, R // 2, HALF), F32),
            vmem((8, R // 2, HALF), F32),
            vmem((8, R // 2, HALF), F32),
            vmem((R, R), F32),
            many(7),
            one, one,
            one, many(4),
            one, one,
            one, one,
            one, many(CHIPS),
            one, one,
            one, one,
            one, one,
            one, one,
            one, one,
            one, one,
            one, one,
        ],
        compiler_params=pltpu.CompilerParams(
            collective_id=0, has_side_effects=True, vmem_limit_bytes=60 * 1024 * 1024
        ),
    )(grad_out[0], hidden[0], error[0], q_init.T)
    return basis.T, q_new.T


def solution(mesh):
    return jax.shard_map(
        body,
        mesh=mesh,
        in_specs=(
            P("dp", "tensor", None),
            P("dp", None, "tensor"),
            P("dp", None, "tensor"),
            P("tensor", None),
        ),
        out_specs=(P("tensor", None), P("tensor", None)),
        check_vma=False,
    )
```
